32 devices in a mesh: row: 8 (over z, core), col: 4 (over y, x).
Axes of the slice: x: 2, y: 2, z: 4, core: 2. Of those that a mesh axis runs over, the one named last changes fastest.
Arguments:
- amplitudes: float32 [2048, 2048], P('row', 'col'), may hold values from -6 to 6
- factor: float32 [2048, 512], P('col'), may hold values from -1.2 to 1.2
- denominators: float32 [2048, 2048], P('row', 'col'), may hold values from 1 to 4
Outputs:
- new_amplitudes: float32 [2048, 2048], P('row', 'col')
The draws below stay inside these ranges and needn't reach their ends.
All inputs are finite; a program needn't handle non-finite values.
Results may differ from the reference program's by a relative error of at most 0.0001.
Values sent between devices are 32-bit elements; how exact they have to be, the bound alone decides.
A program may use at most 64 MiB of HBM per device.

```python
import math
import jax
import jax.numpy as jnp
from jax import lax

K = 512
ITERS = 2
NT = 2048


def shard_levels(key, dims, cuts, low, top_value):
    gain, own = 1.0, jax.random.fold_in(key, 6)
    for position, blocks in cuts:
        heights = jnp.exp(jax.random.uniform(jax.random.fold_in(own, position), (blocks,), jnp.float32, low / len(cuts), top_value / len(cuts)))
        gain = gain * jnp.repeat(heights, dims[position] // blocks).reshape([-1 if axis == position else 1 for axis in range(len(dims))])
    return gain


def gaussian(stream_key, shape, deviation, most, split=(), dtype=jnp.bfloat16):
    array = jax.random.normal(stream_key, shape, jnp.float32) * deviation
    if len(split) > 0:
        array = shard_levels(stream_key, shape, split, -0.22, 0.18) * array
    return jnp.clip(array, min=-most, max=most).astype(dtype)


def setup_inputs(seed: int = 0) -> dict:
    streams_of = jax.random.split(jax.random.key(seed), 4)
    return {
        "amplitudes": gaussian(streams_of[0], (NT, NT), 1.0, 6.0, ((0, 8), (1, 4)), jnp.float32),
        "factor": gaussian(streams_of[1], (NT, K), 0.2, 1.2, ((0, 4),), jnp.float32),
        "denominators": jnp.clip(jnp.exp(math.log(4.0) - 1.3862944 * jax.random.uniform(streams_of[2], (NT, NT), jnp.float32) ** shard_levels(streams_of[2], (NT, NT), ((0, 8), (1, 4)), -0.2, 0.2)), 1.0, 4.0),
    }


def reference(amplitudes, factor, denominators):
    high = lax.Precision.HIGHEST
    scale = 1.0 / math.sqrt(NT)
    base = jnp.dot(factor, factor.T, precision=high)
    amp = amplitudes
    for step in range(ITERS):
        ymat = jnp.dot(amp, factor, precision=high) * scale
        mixed = jnp.dot(ymat, factor.T, precision=high)
        result = base + jnp.dot(ymat, ymat.T, precision=high) + mixed + mixed.T
        amp = result / denominators
    return amp
```

```python
import functools
import math

import jax
import jax.numpy as jnp
from jax import lax
from jax.experimental import pallas as pl
from jax.experimental.pallas import tpu as pltpu
from jax.sharding import PartitionSpec as P

ITERS = 2
MESH = pl.DeviceIdType.MESH
NN = (((1,), (0,)), ((), ()))
NT = (((1,), (1,)), ((), ()))


def split(value):
    high = value.astype(jnp.bfloat16)
    return high, (value - high.astype(jnp.float32)).astype(jnp.bfloat16)


def product(left, right, dims):
    dot = functools.partial(lax.dot_general, dimension_numbers=dims, preferred_element_type=jnp.float32)
    return dot(left[0], right[0]) + (dot(left[0], right[1]) + dot(left[1], right[0]))


def kernel(nrow, ncol, scale, amp_hbm, fac_hbm, den_hbm, out_ref, amp, fac, den, fac_high, fac_low, part, got, zrow, zcol,
           load_sem, rs_send, rs_recv, ag_send, ag_recv, up_send, down_send, chain_recv, lane_send, lane_recv):
    rows, depth = part.shape[1] * part.shape[2], part.shape[3]
    piece = part.shape[2]
    lanes = nrow // ncol
    r = lax.axis_index("row")
    c = lax.axis_index("col")
    q = r // lanes
    k = r % lanes

    loads = [pltpu.make_async_copy(src, dst, load_sem.at[i])
             for i, (src, dst) in enumerate(((amp_hbm, amp), (fac_hbm, fac), (den_hbm, den)))]
    for load in loads:
        load.start()

    barrier = pltpu.get_barrier_semaphore()

    def greet(row, col):
        pl.semaphore_signal(barrier, inc=1, device_id=(row, col), device_id_type=MESH)

    others = [lax.rem(c + d, ncol) for d in range(1, ncol)]
    mates = [lax.rem(k + d, lanes) for d in range(1, lanes)]
    for j in others:
        greet(r, j)
    for m in mates:
        greet(q * lanes + m, c)

    @pl.when(q > 0)
    def _():
        greet(r - lanes, c)

    @pl.when(q < ncol - 1)
    def _():
        greet(r + lanes, c)

    def remote(src, dst, send, recv, row, col):
        return pltpu.make_async_remote_copy(src_ref=src, dst_ref=dst, send_sem=send, recv_sem=recv,
                                            device_id=(row, col), device_id_type=MESH)

    def reduce_copy(it, j):
        return remote(part.at[it, j], got.at[it, c], rs_send.at[it, j], rs_recv.at[it, c], r, j)

    def reduce_arrival(it, j):
        return remote(part.at[it, j], got.at[it, j], rs_send.at[it, j], rs_recv.at[it, j], r, j)

    def gather_copy(it, j):
        return remote(zrow.at[it, c], zrow.at[it, c], ag_send.at[it, j], ag_recv.at[it, c], r, j)

    def gather_arrival(it, j):
        return remote(zrow.at[it, j], zrow.at[it, j], ag_send.at[it, j], ag_recv.at[it, j], r, j)

    def up_copy(it, j):
        return remote(zcol.at[it, k, j], zcol.at[it, k, j], up_send.at[it, j], chain_recv.at[it, j], r + lanes, c)

    def down_copy(it, j):
        return remote(zcol.at[it, k, j], zcol.at[it, k, j], down_send.at[it, j], chain_recv.at[it, j], r - lanes, c)

    def lane_copy(it, m, j):
        return remote(zcol.at[it, k, j], zcol.at[it, k, j], lane_send.at[it, m, j], lane_recv.at[it, k, j], q * lanes + m, c)

    def lane_arrival(it, m, j):
        return remote(zcol.at[it, m, j], zcol.at[it, m, j], lane_send.at[it, m, j], lane_recv.at[it, m, j], q * lanes + m, c)

    goes_up = jnp.logical_and(q >= c, q < ncol - 1)
    goes_down = jnp.logical_and(q <= c, q > 0)

    loads[1].wait()
    fac_high[...], fac_low[...] = split(fac[...])
    loads[0].wait()
    loads[2].wait()

    for it in range(ITERS):
        value = product(split(amp[...]), (fac_high[...], fac_low[...]), NN) * scale
        here = fac[pl.ds(pl.multiple_of(k * rows, rows), rows), :]
        value = value + jnp.where(q == c, here, 0.0)
        part[it] = value.reshape(ncol, piece, depth)
        if it == 0:
            count = (ncol - 1) + (lanes - 1) + (q > 0).astype(jnp.int32) + (q < ncol - 1).astype(jnp.int32)
            pl.semaphore_wait(barrier, count)
        for j in others:
            reduce_copy(it, j).start()
        total = part[it, c]
        for j in others:
            reduce_arrival(it, j).wait_recv()
            total = total + got[it, j]
        zrow[it, c] = total

        for d, j in enumerate([c] + others):
            @pl.when(q == c)
            def _():
                if d > 0:
                    gather_arrival(it, j).wait_recv()
                zcol[it, k, j] = zrow[it, j]

            @pl.when(q != c)
            def _():
                up_copy(it, j).wait_recv()

            @pl.when(goes_up)
            def _():
                up_copy(it, j).start()

            @pl.when(goes_down)
            def _():
                down_copy(it, j).start()

            for m in mates:
                lane_copy(it, m, j).start()
            if d == 0:
                for jj in others:
                    gather_copy(it, jj).start()

        @pl.when(q != c)
        def _():
            for j in others:
                gather_arrival(it, j).wait_recv()

        for m in mates:
            for j in [c] + others:
                lane_arrival(it, m, j).wait_recv()
        left = split(zrow[it].reshape(rows, depth))
        right = split(zcol[it].reshape(lanes * rows, depth))
        result = product(left, right, NT) / den[...]
        if it < ITERS - 1:
            amp[...] = result
        else:
            out_ref[...] = result

    for it in range(ITERS):
        for j in others:
            reduce_copy(it, j).wait_send()
            gather_copy(it, j).wait_send()
        for j in range(ncol):
            @pl.when(goes_up)
            def _():
                up_copy(it, j).wait_send()

            @pl.when(goes_down)
            def _():
                down_copy(it, j).wait_send()

            for m in mates:
                lane_copy(it, m, j).wait_send()


def solution(mesh):
    nrow, ncol = mesh.shape["row"], mesh.shape["col"]
    lanes = nrow // ncol

    def local(amplitudes, factor, denominators):
        rows, cols = amplitudes.shape
        depth = factor.shape[1]
        piece = rows // ncol
        scale = 1.0 / math.sqrt(rows * nrow)
        dma = pltpu.SemaphoreType.DMA
        return pl.pallas_call(
            functools.partial(kernel, nrow, ncol, scale),
            out_shape=jax.ShapeDtypeStruct((rows, cols), jnp.float32),
            in_specs=[pl.BlockSpec(memory_space=pl.ANY)] * 3,
            out_specs=pl.BlockSpec(memory_space=pltpu.VMEM),
            scratch_shapes=[
                pltpu.VMEM((rows, cols), jnp.float32),
                pltpu.VMEM((cols, depth), jnp.float32),
                pltpu.VMEM((rows, cols), jnp.float32),
                pltpu.VMEM((cols, depth), jnp.bfloat16),
                pltpu.VMEM((cols, depth), jnp.bfloat16),
                pltpu.VMEM((ITERS, ncol, piece, depth), jnp.float32),
                pltpu.VMEM((ITERS, ncol, piece, depth), jnp.float32),
                pltpu.VMEM((ITERS, ncol, piece, depth), jnp.float32),
                pltpu.VMEM((ITERS, lanes, ncol, piece, depth), jnp.float32),
                dma((3,)),
                dma((ITERS, ncol)),
                dma((ITERS, ncol)),
                dma((ITERS, ncol)),
                dma((ITERS, ncol)),
                dma((ITERS, ncol)),
                dma((ITERS, ncol)),
                dma((ITERS, ncol)),
                dma((ITERS, lanes, ncol)),
                dma((ITERS, lanes, ncol)),
            ],
            compiler_params=pltpu.CompilerParams(
                collective_id=0, has_side_effects=True, vmem_limit_bytes=48 * 1024 * 1024
            ),
        )(amplitudes, factor, denominators)

    return jax.shard_map(
        local,
        mesh=mesh,
        in_specs=(P("row", "col"), P("col", None), P("row", "col")),
        out_specs=P("row", "col"),
        check_vma=False,
    )
```

```python
import functools
import math

import jax
import jax.numpy as jnp
from jax import lax
from jax.experimental import pallas as pl
from jax.experimental.pallas import tpu as pltpu
from jax.sharding import PartitionSpec as P

ITERS = 2
GROUPS = 4
OWN_LAG = 1
FAR_LAG = 4
MESH = pl.DeviceIdType.MESH
NN = (((1,), (0,)), ((), ()))
NT = (((1,), (1,)), ((), ()))


def split(value):
    high = value.astype(jnp.bfloat16)
    return high, (value - high.astype(jnp.float32)).astype(jnp.bfloat16)


def product(left, right, dims):
    dot = functools.partial(lax.dot_general, dimension_numbers=dims, preferred_element_type=jnp.float32)
    return dot(left[0], right[0]) + (dot(left[0], right[1]) + dot(left[1], right[0]))


def kernel(nrow, ncol, scale, amp_hbm, fac_hbm, den_hbm, out_ref, amp, fac, den, fac_high, fac_low, part, got, zrow, zcol,
           load_sem, rs_send, rs_recv, ag_send, ag_recv, up_send, down_send, chain_recv, lane_send, lane_recv):
    groups, piece, depth = part.shape[2:]
    rows = ncol * groups * piece
    lanes = nrow // ncol
    r = lax.axis_index("row")
    c = lax.axis_index("col")
    q = r // lanes
    k = r % lanes

    loads = [pltpu.make_async_copy(src, dst, load_sem.at[i])
             for i, (src, dst) in enumerate(((amp_hbm, amp), (fac_hbm, fac), (den_hbm, den)))]
    for load in loads:
        load.start()

    barrier = pltpu.get_barrier_semaphore()

    def greet(row, col):
        pl.semaphore_signal(barrier, inc=1, device_id=(row, col), device_id_type=MESH)

    others = [lax.rem(c + d, ncol) for d in range(1, ncol)]
    mates = [lax.rem(k + d, lanes) for d in range(1, lanes)]
    for j in others:
        greet(r, j)
    for m in mates:
        greet(q * lanes + m, c)

    @pl.when(q > 0)
    def _():
        greet(r - lanes, c)

    @pl.when(q < ncol - 1)
    def _():
        greet(r + lanes, c)

    def remote(src, dst, send, recv, row, col):
        return pltpu.make_async_remote_copy(src_ref=src, dst_ref=dst, send_sem=send, recv_sem=recv,
                                            device_id=(row, col), device_id_type=MESH)

    def reduce_copy(it, j, g):
        return remote(part.at[it, j, g], got.at[it, c, g], rs_send.at[it, j, g], rs_recv.at[it, c, g], r, j)

    def reduce_arrival(it, j, g):
        return remote(part.at[it, j, g], got.at[it, j, g], rs_send.at[it, j, g], rs_recv.at[it, j, g], r, j)

    def gather_copy(it, j, g):
        return remote(zrow.at[it, c, g], zrow.at[it, c, g], ag_send.at[it, j, g], ag_recv.at[it, c, g], r, j)

    def gather_arrival(it, j, g):
        return remote(zrow.at[it, j, g], zrow.at[it, j, g], ag_send.at[it, j, g], ag_recv.at[it, j, g], r, j)

    def up_copy(it, j, g):
        return remote(zcol.at[it, k, j, g], zcol.at[it, k, j, g], up_send.at[it, j, g], chain_recv.at[it, j, g], r + lanes, c)

    def down_copy(it, j, g):
        return remote(zcol.at[it, k, j, g], zcol.at[it, k, j, g], down_send.at[it, j, g], chain_recv.at[it, j, g], r - lanes, c)

    def lane_copy(it, m, j, g):
        return remote(zcol.at[it, k, j, g], zcol.at[it, k, j, g], lane_send.at[it, m, j, g], lane_recv.at[it, k, j, g], q * lanes + m, c)

    def lane_arrival(it, m, j, g):
        return remote(zcol.at[it, m, j, g], zcol.at[it, m, j, g], lane_send.at[it, m, j, g], lane_recv.at[it, m, j, g], q * lanes + m, c)

    goes_up = jnp.logical_and(q >= c, q < ncol - 1)
    goes_down = jnp.logical_and(q <= c, q > 0)

    loads[1].wait()
    fac_high[...], fac_low[...] = split(fac[...])
    loads[0].wait()
    loads[2].wait()

    for it in range(ITERS):
        value = product(split(amp[...]), (fac_high[...], fac_low[...]), NN) * scale
        here = fac[pl.ds(pl.multiple_of(k * rows, rows), rows), :]
        value = value + jnp.where(q == c, here, 0.0)
        part[it] = value.reshape(ncol, groups, piece, depth)
        if it == 0:
            count = (ncol - 1) + (lanes - 1) + (q > 0).astype(jnp.int32) + (q < ncol - 1).astype(jnp.int32)
            pl.semaphore_wait(barrier, count)
        for g in range(groups):
            for j in others:
                reduce_copy(it, j, g).start()

        def own(g):
            total = part[it, c, g]
            for j in others:
                reduce_arrival(it, j, g).wait_recv()
                total = total + got[it, j, g]
            zrow[it, c, g] = total

            @pl.when(q == c)
            def _():
                pass_on(c, g)

            for j in others:
                gather_copy(it, j, g).start()

        def pass_on(j, g):
            @pl.when(q == c)
            def _():
                zcol[it, k, j, g] = zrow[it, j, g]

            @pl.when(goes_up)
            def _():
                up_copy(it, j, g).start()

            @pl.when(goes_down)
            def _():
                down_copy(it, j, g).start()

            for m in mates:
                lane_copy(it, m, j, g).start()

        def from_plane(g):
            for j in others:
                gather_arrival(it, j, g).wait_recv()
                pass_on(j, g)

        def from_chain(g):
            for j in [c] + others:
                up_copy(it, j, g).wait_recv()
                pass_on(j, g)

        for step in range(groups + max(OWN_LAG, FAR_LAG)):
            if step < groups:
                own(step)
            if 0 <= step - OWN_LAG < groups:
                pl.when(q == c)(functools.partial(from_plane, step - OWN_LAG))
            if 0 <= step - FAR_LAG < groups:
                pl.when(q != c)(functools.partial(from_chain, step - FAR_LAG))

        @pl.when(q != c)
        def _():
            for g in range(groups):
                for j in others:
                    gather_arrival(it, j, g).wait_recv()

        for g in range(groups):
            for m in mates:
                for j in [c] + others:
                    lane_arrival(it, m, j, g).wait_recv()
        left = split(zrow[it].reshape(rows, depth))
        right = split(zcol[it].reshape(lanes * rows, depth))
        result = product(left, right, NT) / den[...]
        if it < ITERS - 1:
            amp[...] = result
        else:
            out_ref[...] = result

    for it in range(ITERS):
        for g in range(groups):
            for j in others:
                reduce_copy(it, j, g).wait_send()
                gather_copy(it, j, g).wait_send()
            for j in range(ncol):
                @pl.when(goes_up)
                def _():
                    up_copy(it, j, g).wait_send()

                @pl.when(goes_down)
                def _():
                    down_copy(it, j, g).wait_send()

                for m in mates:
                    lane_copy(it, m, j, g).wait_send()


def solution(mesh):
    nrow, ncol = mesh.shape["row"], mesh.shape["col"]
    lanes = nrow // ncol

    def local(amplitudes, factor, denominators):
        rows, cols = amplitudes.shape
        depth = factor.shape[1]
        groups = math.gcd(GROUPS, rows // ncol // 16)
        piece = rows // ncol // groups
        scale = 1.0 / math.sqrt(rows * nrow)
        dma = pltpu.SemaphoreType.DMA
        return pl.pallas_call(
            functools.partial(kernel, nrow, ncol, scale),
            out_shape=jax.ShapeDtypeStruct((rows, cols), jnp.float32),
            in_specs=[pl.BlockSpec(memory_space=pltpu.HBM)] * 3,
            out_specs=pl.BlockSpec(memory_space=pltpu.VMEM),
            scratch_shapes=[
                pltpu.VMEM((rows, cols), jnp.float32),
                pltpu.VMEM((cols, depth), jnp.float32),
                pltpu.VMEM((rows, cols), jnp.float32),
                pltpu.VMEM((cols, depth), jnp.bfloat16),
                pltpu.VMEM((cols, depth), jnp.bfloat16),
                pltpu.VMEM((ITERS, ncol, groups, piece, depth), jnp.float32),
                pltpu.VMEM((ITERS, ncol, groups, piece, depth), jnp.float32),
                pltpu.VMEM((ITERS, ncol, groups, piece, depth), jnp.float32),
                pltpu.VMEM((ITERS, lanes, ncol, groups, piece, depth), jnp.float32),
                dma((3,)),
                dma((ITERS, ncol, groups)),
                dma((ITERS, ncol, groups)),
                dma((ITERS, ncol, groups)),
                dma((ITERS, ncol, groups)),
                dma((ITERS, ncol, groups)),
                dma((ITERS, ncol, groups)),
                dma((ITERS, ncol, groups)),
                dma((ITERS, lanes, ncol, groups)),
                dma((ITERS, lanes, ncol, groups)),
            ],
            compiler_params=pltpu.CompilerParams(
                collective_id=0, has_side_effects=True, vmem_limit_bytes=48 * 1024 * 1024
            ),
        )(amplitudes, factor, denominators)

    return jax.shard_map(
        local,
        mesh=mesh,
        in_specs=(P("row", "col"), P("col", None), P("row", "col")),
        out_specs=P("row", "col"),
        check_vma=False,
    )
```

```python
import functools
import math

import jax
import jax.numpy as jnp
from jax import lax
from jax.experimental import pallas as pl
from jax.experimental.pallas import tpu as pltpu
from jax.sharding import PartitionSpec as P

ITERS = 2
GROUPS = 4
OWN_LAG = 1
FAR_LAG = 4
MESH = pl.DeviceIdType.MESH
NN = (((1,), (0,)), ((), ()))
NT = (((1,), (1,)), ((), ()))


def split(value):
    high = value.astype(jnp.bfloat16)
    return high, (value - high.astype(jnp.float32)).astype(jnp.bfloat16)


def product(left, right, dims):
    dot = functools.partial(lax.dot_general, dimension_numbers=dims, preferred_element_type=jnp.float32)
    return dot(left[0], right[0]) + (dot(left[0], right[1]) + dot(left[1], right[0]))


def kernel(nrow, ncol, scale, amp_hbm, fac_hbm, den_hbm, out_ref, amp, fac, den, fac_high, fac_low, part, got, zrow, zcol,
           load_sem, rs_send, rs_recv, ag_send, ag_recv, up_send, down_send, chain_recv, lane_send, lane_recv):
    groups, piece, depth = part.shape[2:]
    rows = ncol * groups * piece
    lanes = nrow // ncol
    r = lax.axis_index("row")
    c = lax.axis_index("col")
    q = r // lanes
    k = r % lanes

    loads = [pltpu.make_async_copy(src, dst, load_sem.at[i])
             for i, (src, dst) in enumerate(((amp_hbm, amp), (fac_hbm, fac), (den_hbm, den)))]
    for load in loads:
        load.start()

    barrier = pltpu.get_barrier_semaphore()

    def greet(row, col):
        pl.semaphore_signal(barrier, inc=1, device_id=(row, col), device_id_type=MESH)

    others = [lax.rem(c + d, ncol) for d in range(1, ncol)]
    mates = [lax.rem(k + d, lanes) for d in range(1, lanes)]
    for j in others:
        greet(r, j)
    for m in mates:
        greet(q * lanes + m, c)

    @pl.when(q > 0)
    def _():
        greet(r - lanes, c)

    @pl.when(q < ncol - 1)
    def _():
        greet(r + lanes, c)

    def remote(src, dst, send, recv, row, col):
        return pltpu.make_async_remote_copy(src_ref=src, dst_ref=dst, send_sem=send, recv_sem=recv,
                                            device_id=(row, col), device_id_type=MESH)

    def reduce_copy(it, j, g):
        return remote(part.at[it, j, g], got.at[it, c, g], rs_send.at[it, j, g], rs_recv.at[it, c, g], r, j)

    def reduce_arrival(it, j, g):
        return remote(part.at[it, j, g], got.at[it, j, g], rs_send.at[it, j, g], rs_recv.at[it, j, g], r, j)

    def gather_copy(it, j, g):
        return remote(zrow.at[it, c, g], zrow.at[it, c, g], ag_send.at[it, j, g], ag_recv.at[it, c, g], r, j)

    def gather_arrival(it, j, g):
        return remote(zrow.at[it, j, g], zrow.at[it, j, g], ag_send.at[it, j, g], ag_recv.at[it, j, g], r, j)

    def up_copy(it, j, g):
        return remote(zcol.at[it, k, j, g], zcol.at[it, k, j, g], up_send.at[it, j, g], chain_recv.at[it, j, g], r + lanes, c)

    def down_copy(it, j, g):
        return remote(zcol.at[it, k, j, g], zcol.at[it, k, j, g], down_send.at[it, j, g], chain_recv.at[it, j, g], r - lanes, c)

    def lane_copy(it, m, j, g):
        return remote(zcol.at[it, k, j, g], zcol.at[it, k, j, g], lane_send.at[it, m, j, g], lane_recv.at[it, k, j, g], q * lanes + m, c)

    def lane_arrival(it, m, j, g):
        return remote(zcol.at[it, m, j, g], zcol.at[it, m, j, g], lane_send.at[it, m, j, g], lane_recv.at[it, m, j, g], q * lanes + m, c)

    goes_up = jnp.logical_and(q >= c, q < ncol - 1)
    goes_down = jnp.logical_and(q <= c, q > 0)

    loads[1].wait()
    fac_high[...], fac_low[...] = split(fac[...])
    loads[0].wait()
    loads[2].wait()

    for it in range(ITERS):
        value = product(split(amp[...]), (fac_high[...], fac_low[...]), NN) * scale
        here = fac[pl.ds(pl.multiple_of(k * rows, rows), rows), :]
        value = value + jnp.where(q == c, here, 0.0)
        part[it] = value.reshape(ncol, groups, piece, depth)
        if it == 0:
            count = (ncol - 1) + (lanes - 1) + (q > 0).astype(jnp.int32) + (q < ncol - 1).astype(jnp.int32)
            pl.semaphore_wait(barrier, count)
        for g in range(groups):
            for j in others:
                reduce_copy(it, j, g).start()

        def own(g):
            total = part[it, c, g]
            for j in others:
                reduce_arrival(it, j, g).wait_recv()
                total = total + got[it, j, g]
            zrow[it, c, g] = total

            @pl.when(q == c)
            def _():
                pass_on(c, g)

            for j in others:
                pl.when(j == q)(gather_copy(it, j, g).start)

        def rest():
            for g in range(groups):
                for j in others:
                    pl.when(j != q)(gather_copy(it, j, g).start)

        def pass_on(j, g):
            @pl.when(q == c)
            def _():
                zcol[it, k, j, g] = zrow[it, j, g]

            @pl.when(goes_up)
            def _():
                up_copy(it, j, g).start()

            @pl.when(goes_down)
            def _():
                down_copy(it, j, g).start()

            for m in mates:
                lane_copy(it, m, j, g).start()

        def from_plane(g):
            for j in others:
                gather_arrival(it, j, g).wait_recv()
                pass_on(j, g)

        def from_chain(g):
            for j in [c] + others:
                up_copy(it, j, g).wait_recv()
                pass_on(j, g)

        for step in range(groups + max(OWN_LAG, FAR_LAG)):
            if step < groups:
                own(step)
            if step == groups - 1:
                rest()
            if 0 <= step - OWN_LAG < groups:
                pl.when(q == c)(functools.partial(from_plane, step - OWN_LAG))
            if 0 <= step - FAR_LAG < groups:
                pl.when(q != c)(functools.partial(from_chain, step - FAR_LAG))

        @pl.when(q != c)
        def _():
            for g in range(groups):
                for j in others:
                    gather_arrival(it, j, g).wait_recv()

        for g in range(groups):
            for m in mates:
                for j in [c] + others:
                    lane_arrival(it, m, j, g).wait_recv()
        left = split(zrow[it].reshape(rows, depth))
        right = split(zcol[it].reshape(lanes * rows, depth))
        result = product(left, right, NT) / den[...]
        if it < ITERS - 1:
            amp[...] = result
        else:
            out_ref[...] = result

    for it in range(ITERS):
        for g in range(groups):
            for j in others:
                reduce_copy(it, j, g).wait_send()
                gather_copy(it, j, g).wait_send()
            for j in range(ncol):
                @pl.when(goes_up)
                def _():
                    up_copy(it, j, g).wait_send()

                @pl.when(goes_down)
                def _():
                    down_copy(it, j, g).wait_send()

                for m in mates:
                    lane_copy(it, m, j, g).wait_send()


def solution(mesh):
    nrow, ncol = mesh.shape["row"], mesh.shape["col"]
    lanes = nrow // ncol

    def local(amplitudes, factor, denominators):
        rows, cols = amplitudes.shape
        depth = factor.shape[1]
        groups = math.gcd(GROUPS, rows // ncol // 16)
        piece = rows // ncol // groups
        scale = 1.0 / math.sqrt(rows * nrow)
        dma = pltpu.SemaphoreType.DMA
        return pl.pallas_call(
            functools.partial(kernel, nrow, ncol, scale),
            out_shape=jax.ShapeDtypeStruct((rows, cols), jnp.float32),
            in_specs=[pl.BlockSpec(memory_space=pltpu.HBM)] * 3,
            out_specs=pl.BlockSpec(memory_space=pltpu.VMEM),
            scratch_shapes=[
                pltpu.VMEM((rows, cols), jnp.float32),
                pltpu.VMEM((cols, depth), jnp.float32),
                pltpu.VMEM((rows, cols), jnp.float32),
                pltpu.VMEM((cols, depth), jnp.bfloat16),
                pltpu.VMEM((cols, depth), jnp.bfloat16),
                pltpu.VMEM((ITERS, ncol, groups, piece, depth), jnp.float32),
                pltpu.VMEM((ITERS, ncol, groups, piece, depth), jnp.float32),
                pltpu.VMEM((ITERS, ncol, groups, piece, depth), jnp.float32),
                pltpu.VMEM((ITERS, lanes, ncol, groups, piece, depth), jnp.float32),
                dma((3,)),
                dma((ITERS, ncol, groups)),
                dma((ITERS, ncol, groups)),
                dma((ITERS, ncol, groups)),
                dma((ITERS, ncol, groups)),
                dma((ITERS, ncol, groups)),
                dma((ITERS, ncol, groups)),
                dma((ITERS, ncol, groups)),
                dma((ITERS, lanes, ncol, groups)),
                dma((ITERS, lanes, ncol, groups)),
            ],
            compiler_params=pltpu.CompilerParams(
                collective_id=0, has_side_effects=True, vmem_limit_bytes=48 * 1024 * 1024
            ),
        )(amplitudes, factor, denominators)

    return jax.shard_map(
        local,
        mesh=mesh,
        in_specs=(P("row", "col"), P("col", None), P("row", "col")),
        out_specs=P("row", "col"),
        check_vma=False,
    )
```
